512 devices in a mesh: section: 4 (over x), dom: 128 (over y, z, core).
Axes of the slice: x: 4, y: 8, z: 8, core: 2. Of those that a mesh axis runs over, the one named last changes fastest.
Arguments:
- stacked: bfloat16 [4, 16384, 1024], P('section', 'dom'), may hold values from -6 to 6
- edges: int32 [16384, 256], P('dom'), may hold values 0 or 1
- picks: int32 [256, 3], P('dom'), may hold values from 0 to 2
- self_w: bfloat16 [4, 1024, 1024], P('section'), may hold values from -0.1875 to 0.1875
- neigh_w: bfloat16 [4, 1024, 1024], P('section'), may hold values from -0.75 to 0.75
Outputs:
- embeddings: bfloat16 [4, 16384, 1024], P('section', 'dom')
The draws below stay inside these ranges and needn't reach their ends.
Inputs may be any that keep to these rules, and one draw needn't show every extreme that they name: `picks`: A value of 2 means that the destination block has no tile from that direction; smaller values name a slab of the peer partition.
All inputs are finite; a program needn't handle non-finite values. No bound on the sum of `edges` on one device may be relied on, other than what follows from the above.
Results may differ from the reference program's by a relative error of at most 0.006.
Values may be sent and summed in bfloat16 or wider, within the bound.
No kernel may reach another device: no remote copies, remote signals or barrier semaphores. Data moves between devices by JAX's collectives and lax.ppermute only.
A program may use at most 64 MiB of HBM per device.

```python
import jax
import jax.numpy as jnp

D = 1024
BLOCK = 64
SLABS = 2
LAYERS = 4
NODES = 16384
N_DOM = 128


def place_ends(entries, rng, low, high):
    longest = entries.shape.index(max(entries.shape))
    spots = []
    for shift in (0, 1):
        where = [jax.random.randint(jax.random.fold_in(rng, axis), (), 0, length) for axis, length in enumerate(entries.shape)]
        where[longest] = (where[longest] + shift) % entries.shape[longest]
        spots.append(tuple(where))
    return entries.at[spots[0]].set(low).at[spots[1]].set(high)


def levels(stream_key, extent, cuts, smallest, top_value):
    level = 1.0
    for dim, blocks in cuts:
        heights = jax.random.uniform(jax.random.fold_in(jax.random.fold_in(stream_key, 6), dim), (blocks,), jnp.float32, smallest / len(cuts), top_value / len(cuts))
        level = level * jnp.repeat(jnp.exp(heights), extent[dim] // blocks).reshape((-1,) + (1,) * (len(extent) - 1 - dim))
    return level


def gaussian(rng, shape, width, most, pieces=(), held_as=jnp.bfloat16):
    entries = jax.random.normal(rng, shape, jnp.float32) * width
    if len(pieces) > 0:
        entries = levels(rng, shape, pieces, -0.22, 0.18) * entries
    return jnp.clip(entries, min=-most, max=most).astype(held_as)


def setup_inputs(seed: int = 0) -> dict:
    arg_keys = jax.random.split(jax.random.key(seed), 6)
    stacked = gaussian(arg_keys[0], (LAYERS, NODES, D), 1.0, 6.0, ((0, 4), (1, 128)))
    edges = place_ends((jax.random.randint(arg_keys[1], (NODES, 4 * BLOCK), 0, 16) < 1).astype(jnp.int32), jax.random.fold_in(arg_keys[1], 1), 0, 1)
    picks = place_ends(jax.random.randint(arg_keys[2], (NODES // BLOCK, 3), 0, SLABS + 1), jax.random.fold_in(arg_keys[2], 1), 0, SLABS).astype(jnp.int32)
    self_w = gaussian(arg_keys[3], (LAYERS, D, D), D ** -0.5, 0.1875, ((0, 4),))
    neigh_w = gaussian(arg_keys[4], (LAYERS, D, D), (D // 16) ** -0.5, 0.75, ((0, 4),))
    return {"stacked": stacked, "edges": edges, "picks": picks, "self_w": self_w, "neigh_w": neigh_w}


def reference(stacked, edges, picks, self_w, neigh_w):
    layer_count = stacked.shape[0]
    node_total = stacked.shape[1]
    feature_width = stacked.shape[2]
    partitions = N_DOM
    peer_offsets = (-1, 1, 2)
    tile_table = edges.reshape(partitions, SLABS, BLOCK, 4, BLOCK)
    pick_table = picks.reshape(partitions, SLABS, 3)
    live_tiles = (pick_table < SLABS).astype(jnp.float32)
    clamped = jnp.minimum(pick_table, SLABS - 1).astype(jnp.int32)
    partition_ids = jnp.arange(partitions).astype(jnp.int32)
    current = stacked[0].reshape(partitions, SLABS, BLOCK, feature_width)
    results = []
    for layer_index in range(layer_count):
        history = stacked[layer_index].reshape(partitions, SLABS, BLOCK, feature_width)
        produced = []
        for slab_now in range(SLABS):
            fresh_mask = (jnp.arange(SLABS) <= slab_now)[None, :, None, None]
            source = jnp.where(fresh_mask, current, history)
            own_rows = current[:, slab_now]
            tile_zero = tile_table[:, slab_now, :, 0, :].astype(jnp.float32)
            summed = jnp.einsum("pij,pjd->pid", tile_zero, own_rows.astype(jnp.float32))
            degree = 1.0 + jnp.sum(tile_zero, axis=-1)
            for position in range(3):
                peer_field = jnp.roll(source, -peer_offsets[position], axis=0)
                blocks = peer_field[partition_ids, clamped[:, slab_now, position]]
                tile_mask = tile_table[:, slab_now, :, position + 1, :].astype(jnp.float32)
                tile_mask = tile_mask * live_tiles[:, slab_now, position][:, None, None]
                summed = summed + jnp.einsum("pij,pjd->pid", tile_mask, blocks.astype(jnp.float32))
                degree = degree + jnp.sum(tile_mask, axis=-1)
            mean_rows = (summed / degree[..., None]).astype(jnp.bfloat16)
            hidden = jnp.dot(own_rows.reshape(-1, feature_width), self_w[layer_index], preferred_element_type=jnp.float32)
            hidden = hidden + jnp.dot(mean_rows.reshape(-1, feature_width), neigh_w[layer_index], preferred_element_type=jnp.float32)
            produced.append(jnp.maximum(hidden, 0.0).astype(jnp.bfloat16).reshape(partitions, BLOCK, feature_width))
        current = jnp.stack(produced, axis=1)
        results.append(current.reshape(node_total, feature_width))
    return jnp.stack(results)
```

```python
import functools

import jax
import jax.numpy as jnp
from jax import lax
from jax.experimental import pallas as pl
from jax.experimental.pallas import tpu as pltpu
from jax.sharding import PartitionSpec as P

BLOCK = 64
TILES = 4
VMEM = pl.BlockSpec(memory_space=pltpu.VMEM)
SMEM = pl.BlockSpec(memory_space=pltpu.SMEM)
ANY = pl.BlockSpec(memory_space=pl.ANY)


def params():
    return pltpu.CompilerParams(vmem_limit_bytes=32 * 1024 * 1024)


def mask_kernel(where_ref, picks_ref, edges_ref, mask_ref, degree_ref):
    odd = where_ref[1] == 1
    for slab in range(2):
        rows = pl.ds(slab * BLOCK, BLOCK)
        e = edges_ref[rows, :].astype(jnp.float32)
        tiles = [e[:, t * BLOCK : (t + 1) * BLOCK] for t in range(TILES)]
        pick = [picks_ref[slab, k] for k in range(3)]
        behind, ahead, ahead2 = tiles[1], tiles[2], tiles[3]
        swap = jnp.where(odd, behind, ahead)
        cross = jnp.where(odd, ahead, behind)
        swap_pick = jnp.where(odd, pick[0], pick[1])
        cross_pick = jnp.where(odd, pick[1], pick[0])
        peers = ((swap, swap_pick), (cross, cross_pick), (ahead2, pick[2]))
        columns = [tiles[0]]
        for wanted in range(2):
            for tile, p in peers:
                columns.append(tile * jnp.where(p == wanted, 1.0, 0.0))
        columns.append(jnp.zeros_like(tiles[0]))
        full = jnp.concatenate(columns, axis=1)
        mask_ref[rows, :] = full.astype(jnp.bfloat16)
        degree = 1.0 + jnp.sum(full, axis=1, keepdims=True)
        degree_ref[rows, :] = jnp.broadcast_to(degree, (BLOCK, 128))


def self_kernel(layer, row, where_ref, own_ref, weight_ref, out_ref):
    @pl.when(where_ref[0] == layer)
    def _():
        out_ref[...] = jnp.dot(
            own_ref[pl.ds(row, BLOCK), :], weight_ref[...], preferred_element_type=jnp.float32
        )


def layer_kernel(layer, slab, rows, first, *refs):
    where_ref, mask_ref, degree_ref, self_ref, weight_ref = refs[:5]
    sources = refs[5:12]
    if first:
        made_ref, result_ref, sem = refs[12:]
    else:
        made_ref, result_ref, sem = refs[13:]

    @pl.when(where_ref[0] == layer)
    def _():
        mine = pl.ds(slab * BLOCK, BLOCK)
        gathered = jnp.concatenate(
            [ref[pl.ds(row, BLOCK), :] for ref, row in zip(sources, rows)], axis=0
        )
        summed = jnp.dot(
            mask_ref[mine, : 7 * BLOCK], gathered, preferred_element_type=jnp.float32
        )
        mean_rows = (summed / degree_ref[mine, :1]).astype(jnp.bfloat16)
        hidden = self_ref[...] + jnp.dot(
            mean_rows, weight_ref[...], preferred_element_type=jnp.float32
        )
        made_ref[...] = jnp.maximum(hidden, 0.0).astype(jnp.bfloat16)
        copy = pltpu.make_async_copy(made_ref, result_ref.at[mine, :], sem)
        copy.start()
        copy.wait()


def per_device(stacked, edges, picks, self_w, neigh_w):
    layers, domains = lax.axis_size("section"), lax.axis_size("dom")
    width = stacked.shape[2]
    features = stacked[0]
    weight_self, weight_neigh = self_w[0], neigh_w[0]
    section = lax.axis_index("section")
    domain = lax.axis_index("dom")
    where = jnp.stack([section, domain % 2]).astype(jnp.int32)
    axes = ("section", "dom")
    everyone = range(domains)

    def route(value, jumps, sections, hop):
        pairs = [
            (s * domains + (d + jump) % domains, (s + hop) * domains + d)
            for s in sections
            for d in everyone
            for jump in jumps(d)
        ]
        return lax.ppermute(value, axes, pairs)

    def here(d):
        return (0,)

    def swapped(d):
        return (1,) if d % 2 == 0 else (-1,)

    def crossed(d):
        return (-1,) if d % 2 == 0 else (1,)

    def up2(d):
        return (2,)

    mask, degree = pl.pallas_call(
        mask_kernel,
        out_shape=(
            jax.ShapeDtypeStruct((2 * BLOCK, 8 * BLOCK), jnp.bfloat16),
            jax.ShapeDtypeStruct((2 * BLOCK, 128), jnp.float32),
        ),
        in_specs=[SMEM, SMEM, VMEM],
        out_specs=(VMEM, VMEM),
        compiler_params=params(),
        name="masks",
    )(where, picks, edges)

    def self_part(layer, own, row):
        return pl.pallas_call(
            functools.partial(self_kernel, layer, row),
            out_shape=jax.ShapeDtypeStruct((BLOCK, width), jnp.float32),
            in_specs=[SMEM, VMEM, VMEM],
            out_specs=VMEM,
            compiler_params=params(),
            cost_estimate=pl.CostEstimate(
                flops=2 * BLOCK * width * width, bytes_accessed=2 * width * width, transcendentals=0
            ),
            name="self_part",
        )(where, own, weight_self)

    def layer_part(layer, slab, sources, part, result):
        arrays, rows = zip(*sources)
        first = result is None
        extra = () if first else (result,)
        return pl.pallas_call(
            functools.partial(layer_kernel, layer, slab, rows, first),
            out_shape=(
                jax.ShapeDtypeStruct((BLOCK, width), jnp.bfloat16),
                jax.ShapeDtypeStruct((2 * BLOCK, width), jnp.bfloat16),
            ),
            in_specs=[SMEM] + [VMEM] * 11 + [ANY] * len(extra),
            out_specs=(VMEM, ANY),
            scratch_shapes=[pltpu.SemaphoreType.DMA],
            input_output_aliases={} if first else {12: 1},
            compiler_params=params(),
            cost_estimate=pl.CostEstimate(
                flops=4 * BLOCK * width * width, bytes_accessed=2 * width * width, transcendentals=0
            ),
            name="layer_part",
        )(where, mask, degree, part, weight_neigh, *arrays, *extra)

    staged = [route(features, jumps, range(layers), 0) for jumps in (up2, crossed, swapped)][::-1]
    old = [[(array, slab * BLOCK) for array in staged] for slab in range(2)]
    own = [(features, 0), (features, BLOCK)]
    fresh = old
    result = None
    for layer in range(layers):
        made = []
        incoming = []
        for slab in range(2):
            if layer:
                own_now, peers_now = arriving[slab]
                swap = route(own_now, swapped, [layer], 0)
                own[slab] = (own_now, 0)
                fresh[slab] = [(swap, 0)] + [(array, 0) for array in peers_now]
            part = self_part(layer, *own[slab])
            second = fresh[1] if slab == 1 else old[1]
            produced, result = layer_part(
                layer, slab, [own[slab]] + fresh[0] + second, part, result
            )
            if layer < layers - 1:
                sent = [route(produced, jumps, [layer], 1) for jumps in (here, crossed, up2)]
                incoming.append((sent[0], sent[1:]))
        arriving = incoming
        fresh = [None, None]
    return result[None]


def solution(mesh):
    in_specs = (
        P("section", "dom", None),
        P("dom", None),
        P("dom", None),
        P("section", None, None),
        P("section", None, None),
    )
    out_specs = P("section", "dom", None)
    return jax.shard_map(
        per_device, mesh=mesh, in_specs=in_specs, out_specs=out_specs, check_vma=False
    )
```

```python
import functools

import jax
import jax.numpy as jnp
from jax import lax
from jax.experimental import pallas as pl
from jax.experimental.pallas import tpu as pltpu
from jax.sharding import PartitionSpec as P

BLOCK = 64
TILES = 4
VMEM = pl.BlockSpec(memory_space=pltpu.VMEM)
SMEM = pl.BlockSpec(memory_space=pltpu.SMEM)
ANY = pl.BlockSpec(memory_space=pl.ANY)


def params():
    return pltpu.CompilerParams(vmem_limit_bytes=32 * 1024 * 1024)


def mask_kernel(where_ref, picks_ref, edges_ref, mask_ref, degree_ref):
    odd = where_ref[1] == 1
    for slab in range(2):
        rows = pl.ds(slab * BLOCK, BLOCK)
        e = edges_ref[rows, :].astype(jnp.float32)
        tiles = [e[:, t * BLOCK : (t + 1) * BLOCK] for t in range(TILES)]
        pick = [picks_ref[slab, k] for k in range(3)]
        behind, ahead, ahead2 = tiles[1], tiles[2], tiles[3]
        swap = jnp.where(odd, behind, ahead)
        cross = jnp.where(odd, ahead, behind)
        swap_pick = jnp.where(odd, pick[0], pick[1])
        cross_pick = jnp.where(odd, pick[1], pick[0])
        peers = ((ahead2, pick[2]), (cross, cross_pick), (swap, swap_pick))
        columns = [tiles[0]]
        for wanted in range(2):
            for tile, p in peers:
                columns.append(tile * jnp.where(p == wanted, 1.0, 0.0))
        columns.append(jnp.zeros_like(tiles[0]))
        full = jnp.concatenate(columns, axis=1)
        mask_ref[rows, :] = full.astype(jnp.bfloat16)
        degree = 1.0 + jnp.sum(full, axis=1, keepdims=True)
        degree_ref[rows, :] = jnp.broadcast_to(degree, (BLOCK, 128))


def self_kernel(layer, row, where_ref, own_ref, weight_ref, out_ref):
    @pl.when(where_ref[0] == layer)
    def _():
        out_ref[...] = jnp.dot(
            own_ref[pl.ds(row, BLOCK), :], weight_ref[...], preferred_element_type=jnp.float32
        )


def product(slab, rows, refs):
    mask_ref, degree_ref, self_ref, weight_ref = refs[:4]
    mine = pl.ds(slab * BLOCK, BLOCK)
    gathered = jnp.concatenate(
        [ref[pl.ds(row, BLOCK), :] for ref, row in zip(refs[4:], rows)], axis=0
    )
    summed = jnp.dot(
        mask_ref[mine, : 7 * BLOCK], gathered, preferred_element_type=jnp.float32
    )
    mean_rows = (summed / degree_ref[mine, :1]).astype(jnp.bfloat16)
    hidden = self_ref[...] + jnp.dot(
        mean_rows, weight_ref[...], preferred_element_type=jnp.float32
    )
    return jnp.maximum(hidden, 0.0).astype(jnp.bfloat16)


def layer_kernel(layer, slab, rows, where_ref, *refs):
    @pl.when(where_ref[0] == layer)
    def _():
        refs[-1][...] = product(slab, rows, refs[:11])


def last_kernel(layer, rows, where_ref, *refs):
    made = refs[11:-3]
    result_ref, block_ref, sems = refs[-3:]

    def leave(source, slab):
        return pltpu.make_async_copy(
            source, result_ref.at[pl.ds(slab * BLOCK, BLOCK), :], sems.at[slab]
        )

    for earlier in range(layer):

        @pl.when(where_ref[0] == earlier)
        def _():
            copies = [leave(made[2 * earlier + slab], slab) for slab in range(2)]
            for copy in copies:
                copy.start()
            for copy in copies:
                copy.wait()

    @pl.when(where_ref[0] == layer)
    def _():
        before = leave(made[2 * layer], 0)
        before.start()
        block_ref[...] = product(1, rows, refs[:11])
        after = leave(block_ref, 1)
        after.start()
        before.wait()
        after.wait()


def per_device(stacked, edges, picks, self_w, neigh_w):
    layers, domains = lax.axis_size("section"), lax.axis_size("dom")
    width = stacked.shape[2]
    features = stacked[0]
    weight_self, weight_neigh = self_w[0], neigh_w[0]
    section = lax.axis_index("section")
    domain = lax.axis_index("dom")
    where = jnp.stack([section, domain % 2]).astype(jnp.int32)
    axes = ("section", "dom")
    everyone = range(domains)

    def route(value, jumps, sections, hop, label):
        pairs = [
            (s * domains + (d + jump) % domains, (s + hop) * domains + d)
            for s in sections
            for d in everyone
            for jump in jumps(d)
        ]
        with jax.named_scope(label):
            return lax.ppermute(value, axes, pairs)

    def here(d):
        return (0,)

    def swapped(d):
        return (1,) if d % 2 == 0 else (-1,)

    def crossed(d):
        return (-1,) if d % 2 == 0 else (1,)

    def up2(d):
        return (2,)

    mask, degree = pl.pallas_call(
        mask_kernel,
        out_shape=(
            jax.ShapeDtypeStruct((2 * BLOCK, 8 * BLOCK), jnp.bfloat16),
            jax.ShapeDtypeStruct((2 * BLOCK, 128), jnp.float32),
        ),
        in_specs=[SMEM, SMEM, VMEM],
        out_specs=(VMEM, VMEM),
        compiler_params=params(),
        name="masks",
    )(where, picks, edges)

    cost = pl.CostEstimate(flops=1_000_000_000, bytes_accessed=0, transcendentals=0)

    def self_part(layer, own, row):
        return pl.pallas_call(
            functools.partial(self_kernel, layer, row),
            out_shape=jax.ShapeDtypeStruct((BLOCK, width), jnp.float32),
            in_specs=[SMEM, VMEM, VMEM],
            out_specs=VMEM,
            compiler_params=params(),
            cost_estimate=cost,
            name="self_part",
        )(where, own, weight_self)

    def layer_part(layer, slab, sources, part):
        arrays, rows = zip(*sources)
        return pl.pallas_call(
            functools.partial(layer_kernel, layer, slab, rows),
            out_shape=jax.ShapeDtypeStruct((BLOCK, width), jnp.bfloat16),
            in_specs=[SMEM] + [VMEM] * 11,
            out_specs=VMEM,
            compiler_params=params(),
            cost_estimate=cost,
            name="layer_part",
        )(where, mask, degree, part, weight_neigh, *arrays)

    def last_part(layer, sources, part, made):
        arrays, rows = zip(*sources)
        return pl.pallas_call(
            functools.partial(last_kernel, layer, rows),
            out_shape=jax.ShapeDtypeStruct((2 * BLOCK, width), jnp.bfloat16),
            in_specs=[SMEM] + [VMEM] * (11 + len(made)),
            out_specs=ANY,
            scratch_shapes=[
                pltpu.VMEM((BLOCK, width), jnp.bfloat16),
                pltpu.SemaphoreType.DMA((2,)),
            ],
            compiler_params=params(),
            cost_estimate=cost,
            name="last_part",
        )(where, mask, degree, part, weight_neigh, *arrays, *made)

    staged = [
        route(features, jumps, range(layers), 0, "init_" + jumps.__name__)
        for jumps in (up2, crossed, swapped)
    ]
    old = [[(array, slab * BLOCK) for array in staged] for slab in range(2)]
    made = []
    for layer in range(layers):
        incoming = []
        fresh = [old[0], None]
        for slab in range(2):
            if layer:
                own_now, peers_now = arriving[slab]
                if slab:
                    own_now, _ = lax.optimization_barrier((own_now, made[-1]))
                swap = route(own_now, swapped, [layer], 0, f"swap_l{layer}s{slab}")
                own = (own_now, 0)
                fresh[slab] = [(array, 0) for array in peers_now + [swap]]
            else:
                own = (features, slab * BLOCK)
                fresh[slab] = old[slab]
            with jax.named_scope(f"self_l{layer}s{slab}"):
                part = self_part(layer, *own)
            second = fresh[1] if slab == 1 else old[1]
            sources = [own] + fresh[0] + second
            with jax.named_scope(f"layer_l{layer}s{slab}"):
                if layer == layers - 1 and slab == 1:
                    result = last_part(layer, sources, part, made)
                else:
                    made.append(layer_part(layer, slab, sources, part))
            if layer < layers - 1:
                sent = [
                    route(made[-1], jumps, [layer], 1, f"{jumps.__name__}_l{layer}s{slab}")
                    for jumps in (here, up2, crossed)
                ]
                incoming.append((sent[0], sent[1:]))
        arriving = incoming
    return result[None]


def solution(mesh):
    in_specs = (
        P("section", "dom", None),
        P("dom", None),
        P("dom", None),
        P("section", None, None),
        P("section", None, None),
    )
    out_specs = P("section", "dom", None)
    return jax.shard_map(
        per_device, mesh=mesh, in_specs=in_specs, out_specs=out_specs, check_vma=False
    )
```

```python
import functools

import jax
import jax.numpy as jnp
from jax import lax
from jax.experimental import pallas as pl
from jax.experimental.pallas import tpu as pltpu
from jax.sharding import PartitionSpec as P

BLOCK = 64
ROWS = 2 * BLOCK
SPAN = 6 * BLOCK
VMEM = pl.BlockSpec(memory_space=pltpu.VMEM)
SMEM = pl.BlockSpec(memory_space=pltpu.SMEM)
ANY = pl.BlockSpec(memory_space=pl.ANY)
COST = pl.CostEstimate(flops=1_000_000_000, bytes_accessed=0, transcendentals=0)


def params():
    return pltpu.CompilerParams(vmem_limit_bytes=32 * 1024 * 1024)


def at(where_ref, section, core):
    return (where_ref[0] == section) & (where_ref[1] == core)


def dot(a, b):
    return jnp.dot(a, b, preferred_element_type=jnp.float32)


def tiles_kernel(picks_ref, edges_ref, tiles_ref):
    for slab in range(2):
        rows = pl.ds(slab * BLOCK, BLOCK)
        e = edges_ref[rows, :].astype(jnp.float32)
        columns = [e[:, :BLOCK]]
        for wanted in range(2):
            for k in range(3):
                live = jnp.where(picks_ref[slab, k] == wanted, 1.0, 0.0)
                columns.append(e[:, (k + 1) * BLOCK : (k + 2) * BLOCK] * live)
        columns.append(jnp.zeros_like(columns[0]))
        tiles_ref[rows, :] = jnp.concatenate(columns, axis=1).astype(jnp.bfloat16)


def weave_kernel(where_ref, mine_ref, other_ref, near_ref, far_ref, lend_ref, degree_ref):
    for core in range(2):
        even_ref, odd_ref = (mine_ref, other_ref) if core == 0 else (other_ref, mine_ref)

        @pl.when(where_ref[1] == core)
        def _():
            def put(out_ref, to_slab, from_slab):
                for r, ref in enumerate((even_ref, odd_ref)):
                    t = ref[pl.ds(to_slab * BLOCK, BLOCK), :].astype(jnp.float32)
                    part = [t[:, i * BLOCK : (i + 1) * BLOCK] for i in range(7)]
                    none = jnp.zeros_like(part[0])
                    behind, ahead, ahead2 = part[1 + 3 * from_slab : 4 + 3 * from_slab]
                    own = part[0] if to_slab == from_slab else none
                    five = [behind, own, ahead, ahead2, none]
                    columns = five + [none] if r == 0 else [none] + five
                    out_ref[pl.ds(r * BLOCK, BLOCK), :] = jnp.concatenate(columns, axis=1).astype(
                        jnp.bfloat16
                    )

            put(near_ref, core, core)
            put(far_ref, core, 1 - core)
            put(lend_ref, 1, 0)
            for r, ref in enumerate((even_ref, odd_ref)):
                t = ref[pl.ds(core * BLOCK, BLOCK), :].astype(jnp.float32)
                degree = 1.0 + jnp.sum(t, axis=1, keepdims=True)
                degree_ref[pl.ds(r * BLOCK, BLOCK), :] = jnp.broadcast_to(degree, (BLOCK, 128))


def staged_rows(core, slab, refs):
    down, mine, other, up_mine, up_other = refs
    if core == 0:
        order = (down, mine, other, up_mine, up_other, down)
    else:
        order = (down, other, mine, up_other, up_mine, down)
    return jnp.concatenate([ref[pl.ds(slab * BLOCK, BLOCK), :] for ref in order], axis=0)


def finish(summed, degree_ref, self_ref, weight_ref):
    mean_rows = (summed / degree_ref[:, :1]).astype(jnp.bfloat16)
    hidden = self_ref[...] + dot(mean_rows, weight_ref[...])
    return jnp.maximum(hidden, 0.0).astype(jnp.bfloat16)


def first_self_kernel(where_ref, weight_ref, mine_ref, other_ref, out_ref):
    for core in range(2):
        even_ref, odd_ref = (mine_ref, other_ref) if core == 0 else (other_ref, mine_ref)

        @pl.when(at(where_ref, 0, core))
        def _():
            rows = pl.ds(core * BLOCK, BLOCK)
            own = jnp.concatenate([even_ref[rows, :], odd_ref[rows, :]], axis=0)
            out_ref[...] = dot(own, weight_ref[...])


def first_kernel(
    core, where_ref, near_ref, far_ref, degree_ref, self_ref, weight_ref, down_ref, mine_ref,
    other_ref, up_mine_ref, up_other_ref, made_ref, tail_ref,
):
    refs = (down_ref, mine_ref, other_ref, up_mine_ref, up_other_ref)

    @pl.when(at(where_ref, 0, core))
    def _():
        summed = dot(near_ref[...], staged_rows(core, core, refs))
        summed = summed + dot(far_ref[...], staged_rows(core, 1 - core, refs))
        made = finish(summed, degree_ref, self_ref, weight_ref)
        made_ref[...] = made
        tail_ref[...] = made[BLOCK:]


def history_kernel(
    where_ref, far_ref, down_ref, mine_ref, other_ref, up_mine_ref, up_other_ref, out_ref
):
    refs = (down_ref, mine_ref, other_ref, up_mine_ref, up_other_ref)

    @pl.when((where_ref[0] > 0) & (where_ref[1] == 0))
    def _():
        out_ref[...] = dot(far_ref[...], staged_rows(0, 1, refs))


def self_kernel(layer, core, where_ref, weight_ref, own_ref, out_ref):
    @pl.when(at(where_ref, layer, core))
    def _():
        out_ref[...] = dot(own_ref[...], weight_ref[...])


def fresh_rows(down_ref, own_ref, up_ref):
    return jnp.concatenate([down_ref[...], own_ref[...], up_ref[...], down_ref[...]], axis=0)


def slab0_kernel(
    layer, where_ref, near_ref, lend_ref, degree_ref, self_ref, base_ref, weight_ref, down_ref,
    own_ref, up_ref, made_ref, tail_ref, lent_ref,
):
    @pl.when(at(where_ref, layer, 0))
    def _():
        rows = fresh_rows(down_ref, own_ref, up_ref)
        summed = dot(near_ref[...], rows) + base_ref[...]
        made = finish(summed, degree_ref, self_ref, weight_ref)
        made_ref[...] = made
        tail_ref[...] = made[BLOCK:]
        lent_ref[...] = dot(lend_ref[...], rows)


def slab1_kernel(
    layer, where_ref, near_ref, degree_ref, self_ref, base_ref, weight_ref, down_ref, own_ref,
    up_ref, made_ref, tail_ref,
):
    @pl.when(at(where_ref, layer, 1))
    def _():
        rows = fresh_rows(down_ref, own_ref, up_ref)
        summed = dot(near_ref[...], rows) + base_ref[...]
        made = finish(summed, degree_ref, self_ref, weight_ref)
        made_ref[...] = made
        tail_ref[...] = made[BLOCK:]


def last_kernel(
    layer, where_ref, near_ref, degree_ref, self_ref, base_ref, weight_ref, down_ref, own_ref,
    up_ref, *refs,
):
    done, (home_ref, away_ref) = refs[:-2], refs[-2:]
    for earlier in range(layer + 1):
        for core in range(2):
            if (earlier, core) == (layer, 1):
                continue
            ref = done[2 * earlier + core]

            @pl.when(at(where_ref, earlier, core))
            def _():
                home_ref[...] = ref[pl.ds(core * BLOCK, BLOCK), :]
                away_ref[...] = ref[pl.ds((1 - core) * BLOCK, BLOCK), :]

    @pl.when(at(where_ref, layer, 1))
    def _():
        rows = fresh_rows(down_ref, own_ref, up_ref)
        summed = dot(near_ref[...], rows) + base_ref[...]
        made = finish(summed, degree_ref, self_ref, weight_ref)
        home_ref[...] = made[BLOCK:]
        away_ref[...] = made[:BLOCK]


def leave_kernel(where_ref, home_ref, arrived_ref, result_ref, sems):
    for core in range(2):

        @pl.when(where_ref[1] == core)
        def _():
            copies = [
                pltpu.make_async_copy(
                    ref, result_ref.at[pl.ds(slab * BLOCK, BLOCK), :], sems.at[slab]
                )
                for slab, ref in ((core, home_ref), (1 - core, arrived_ref))
            ]
            for copy in copies:
                copy.start()
            for copy in copies:
                copy.wait()


def call(kernel, outs, *args, label, **extra):
    options = dict(compiler_params=params(), cost_estimate=COST, name=label)
    options.update(extra)
    specs = [SMEM if a.dtype == jnp.int32 and a.size < 128 else VMEM for a in args]
    options.setdefault("out_specs", [VMEM] * len(outs))
    return pl.pallas_call(kernel, out_shape=outs, in_specs=specs, **options)(*args)


def per_device(stacked, edges, picks, self_w, neigh_w):
    layers, domains = lax.axis_size("section"), lax.axis_size("dom")
    width = stacked.shape[2]
    mine = stacked[0]
    weight_self, weight_neigh = self_w[0], neigh_w[0]
    where = jnp.stack([lax.axis_index("section"), lax.axis_index("dom") % 2]).astype(jnp.int32)

    def bf16(rows, columns=width):
        return jax.ShapeDtypeStruct((rows, columns), jnp.bfloat16)

    def f32(rows, columns=width):
        return jax.ShapeDtypeStruct((rows, columns), jnp.float32)

    def route(value, jump, cores, sections, hop, label):
        pairs = [
            (s * domains + (d + jump(d)) % domains, (s + hop) * domains + d)
            for s in sections
            for d in range(domains)
            if d % 2 in cores
        ]
        with jax.named_scope(label):
            return lax.ppermute(value, ("section", "dom"), pairs)

    def steady(jump):
        return lambda d: jump

    def partner(d):
        return 1 if d % 2 == 0 else -1

    every = range(layers)
    both = (0, 1)
    up_mine = route(mine, steady(2), both, every, 0, "init_up")
    down_even = route(mine, steady(-1), (0,), every, 0, "init_down")
    other = route(mine, partner, both, every, 0, "init_other")
    (tiles,) = call(tiles_kernel, [bf16(ROWS, 8 * BLOCK)], picks, edges, label="tiles")
    tiles_other = route(tiles, partner, both, every, 0, "init_tiles")
    near, far, lend, degree = call(
        weave_kernel,
        [bf16(ROWS, SPAN)] * 3 + [f32(ROWS, 128)],
        where, tiles, tiles_other,
        label="weave",
    )
    (part,) = call(first_self_kernel, [f32(ROWS)], where, weight_self, mine, other, label="self0")
    up_other = route(up_mine, partner, both, every, 0, "init_up_other")
    down_odd = route(down_even, partner, (1,), [0], 0, "init_down_odd")
    made, tail = [], []
    for core in range(2):
        m, t = call(
            functools.partial(first_kernel, core),
            [bf16(ROWS), bf16(BLOCK)],
            where, near, far, degree, part, weight_neigh,
            down_odd if core else down_even, mine, other, up_mine, up_other,
            label="first",
        )
        made.append(m)
        tail.append(t)
    (base,) = call(
        history_kernel, [f32(ROWS)], where, far, down_even, mine, other, up_mine, up_other,
        label="history",
    )
    done = list(made)
    for layer in range(1, layers):
        fresh = []
        for core in range(2):
            cores, ends = (core,), [layer - 1]
            own = route(made[core], steady(0), cores, ends, 1, f"own_l{layer}c{core}")
            up = route(made[core], steady(2), cores, ends, 1, f"up_l{layer}c{core}")
            down = route(tail[core], steady(-2), cores, ends, 1, f"down_l{layer}c{core}")
            with jax.named_scope(f"self_l{layer}c{core}"):
                (part,) = call(
                    functools.partial(self_kernel, layer, core), [f32(ROWS)],
                    where, weight_self, own, label="self",
                )
            fresh.append((part, down, own, up))
        part, down, own, up = fresh[0]
        with jax.named_scope(f"slab0_l{layer}"):
            m0, t0, lent = call(
                functools.partial(slab0_kernel, layer),
                [bf16(ROWS), bf16(BLOCK), f32(ROWS)],
                where, near, lend, degree, part, base, weight_neigh, down, own, up,
                label="slab0",
            )
        lent = route(lent, partner, (1,), [layer], 0, f"lent_l{layer}")
        part, down, own, up = fresh[1]
        inputs = (where, near, degree, part, lent, weight_neigh, down, own, up)
        done.append(m0)
        with jax.named_scope(f"slab1_l{layer}"):
            if layer < layers - 1:
                m1, t1 = call(
                    functools.partial(slab1_kernel, layer), [bf16(ROWS), bf16(BLOCK)], *inputs,
                    label="slab1",
                )
                done.append(m1)
                made, tail = [m0, m1], [t0, t1]
            else:
                home, away = call(
                    functools.partial(last_kernel, layer), [bf16(BLOCK)] * 2, *inputs, *done,
                    label="last",
                )
    arrived = route(away, partner, both, every, 0, "last_swap")
    (result,) = call(
        leave_kernel,
        [bf16(ROWS)],
        where, home, arrived,
        label="leave",
        out_specs=[ANY],
        scratch_shapes=[pltpu.SemaphoreType.DMA((2,))],
    )
    return result[None]


def solution(mesh):
    in_specs = (
        P("section", "dom", None),
        P("dom", None),
        P("dom", None),
        P("section", None, None),
        P("section", None, None),
    )
    out_specs = P("section", "dom", None)
    return jax.shard_map(
        per_device, mesh=mesh, in_specs=in_specs, out_specs=out_specs, check_vma=False
    )
```

```python
import functools

import jax
import jax.numpy as jnp
from jax import lax
from jax.experimental import pallas as pl
from jax.experimental.pallas import tpu as pltpu
from jax.sharding import PartitionSpec as P

BLOCK = 64
ROWS = 2 * BLOCK
SPAN = 6 * BLOCK
VMEM = pl.BlockSpec(memory_space=pltpu.VMEM)
SMEM = pl.BlockSpec(memory_space=pltpu.SMEM)
ANY = pl.BlockSpec(memory_space=pl.ANY)
COST = pl.CostEstimate(flops=1_000_000_000, bytes_accessed=0, transcendentals=0)


def params():
    return pltpu.CompilerParams(vmem_limit_bytes=32 * 1024 * 1024)


def at(where_ref, section, core):
    return (where_ref[0] == section) & (where_ref[1] == core)


def dot(a, b):
    return jnp.dot(a, b, preferred_element_type=jnp.float32)


def tiles_kernel(picks_ref, edges_ref, tiles_ref):
    for slab in range(2):
        rows = pl.ds(slab * BLOCK, BLOCK)
        e = edges_ref[rows, :].astype(jnp.float32)
        columns = [e[:, :BLOCK]]
        for wanted in range(2):
            for k in range(3):
                live = jnp.where(picks_ref[slab, k] == wanted, 1.0, 0.0)
                columns.append(e[:, (k + 1) * BLOCK : (k + 2) * BLOCK] * live)
        columns.append(jnp.zeros_like(columns[0]))
        tiles_ref[rows, :] = jnp.concatenate(columns, axis=1).astype(jnp.bfloat16)


def weave_kernel(where_ref, mine_ref, other_ref, near_ref, far_ref, lend_ref, degree_ref):
    for core in range(2):
        even_ref, odd_ref = (mine_ref, other_ref) if core == 0 else (other_ref, mine_ref)

        @pl.when(where_ref[1] == core)
        def _():
            def put(out_ref, to_slab, from_slab):
                for r, ref in enumerate((even_ref, odd_ref)):
                    t = ref[pl.ds(to_slab * BLOCK, BLOCK), :].astype(jnp.float32)
                    part = [t[:, i * BLOCK : (i + 1) * BLOCK] for i in range(7)]
                    none = jnp.zeros_like(part[0])
                    behind, ahead, ahead2 = part[1 + 3 * from_slab : 4 + 3 * from_slab]
                    own = part[0] if to_slab == from_slab else none
                    five = [behind, own, ahead, ahead2, none]
                    columns = five + [none] if r == 0 else [none] + five
                    out_ref[pl.ds(r * BLOCK, BLOCK), :] = jnp.concatenate(columns, axis=1).astype(
                        jnp.bfloat16
                    )

            put(near_ref, core, core)
            put(far_ref, core, 1 - core)
            put(lend_ref, 1, 0)
            for r, ref in enumerate((even_ref, odd_ref)):
                t = ref[pl.ds(core * BLOCK, BLOCK), :].astype(jnp.float32)
                degree = 1.0 + jnp.sum(t, axis=1, keepdims=True)
                degree_ref[pl.ds(r * BLOCK, BLOCK), :] = jnp.broadcast_to(degree, (BLOCK, 128))


def staged_rows(core, slab, refs):
    down, mine, other, up_mine, up_other = refs
    if core == 0:
        order = (down, mine, other, up_mine, up_other, down)
    else:
        order = (down, other, mine, up_other, up_mine, down)
    return jnp.concatenate([ref[pl.ds(slab * BLOCK, BLOCK), :] for ref in order], axis=0)


def finish(summed, degree_ref, self_ref, weight_ref):
    mean_rows = (summed / degree_ref[:, :1]).astype(jnp.bfloat16)
    hidden = self_ref[...] + dot(mean_rows, weight_ref[...])
    return jnp.maximum(hidden, 0.0).astype(jnp.bfloat16)


def first_self_kernel(where_ref, weight_ref, mine_ref, other_ref, out_ref):
    for core in range(2):
        even_ref, odd_ref = (mine_ref, other_ref) if core == 0 else (other_ref, mine_ref)

        @pl.when(at(where_ref, 0, core))
        def _():
            rows = pl.ds(core * BLOCK, BLOCK)
            own = jnp.concatenate([even_ref[rows, :], odd_ref[rows, :]], axis=0)
            out_ref[...] = dot(own, weight_ref[...])


def first_kernel(
    core, where_ref, near_ref, far_ref, degree_ref, self_ref, weight_ref, down_ref, mine_ref,
    other_ref, up_mine_ref, up_other_ref, made_ref, tail_ref,
):
    refs = (down_ref, mine_ref, other_ref, up_mine_ref, up_other_ref)

    @pl.when(at(where_ref, 0, core))
    def _():
        summed = dot(near_ref[...], staged_rows(core, core, refs))
        summed = summed + dot(far_ref[...], staged_rows(core, 1 - core, refs))
        made = finish(summed, degree_ref, self_ref, weight_ref)
        made_ref[...] = made
        tail_ref[...] = made[BLOCK:]


def history_kernel(
    where_ref, far_ref, down_ref, mine_ref, other_ref, up_mine_ref, up_other_ref, out_ref
):
    refs = (down_ref, mine_ref, other_ref, up_mine_ref, up_other_ref)

    @pl.when((where_ref[0] > 0) & (where_ref[1] == 0))
    def _():
        out_ref[...] = dot(far_ref[...], staged_rows(0, 1, refs))


def self_kernel(layer, core, where_ref, weight_ref, own_ref, out_ref):
    @pl.when(at(where_ref, layer, core))
    def _():
        out_ref[...] = dot(own_ref[...], weight_ref[...])


def fresh_rows(down_ref, own_ref, up_ref):
    return jnp.concatenate([down_ref[...], own_ref[...], up_ref[...], down_ref[...]], axis=0)


def slab0_kernel(
    layer, where_ref, near_ref, lend_ref, degree_ref, self_ref, base_ref, weight_ref, down_ref,
    own_ref, up_ref, made_ref, tail_ref, lent_ref,
):
    @pl.when(at(where_ref, layer, 0))
    def _():
        rows = fresh_rows(down_ref, own_ref, up_ref)
        summed = dot(near_ref[...], rows) + base_ref[...]
        made = finish(summed, degree_ref, self_ref, weight_ref)
        made_ref[...] = made
        tail_ref[...] = made[BLOCK:]
        lent_ref[...] = dot(lend_ref[...], rows)


def slab1_kernel(
    layer, where_ref, near_ref, degree_ref, self_ref, base_ref, weight_ref, down_ref, own_ref,
    up_ref, made_ref, tail_ref,
):
    @pl.when(at(where_ref, layer, 1))
    def _():
        rows = fresh_rows(down_ref, own_ref, up_ref)
        summed = dot(near_ref[...], rows) + base_ref[...]
        made = finish(summed, degree_ref, self_ref, weight_ref)
        made_ref[...] = made
        tail_ref[...] = made[BLOCK:]


def last_kernel(
    layer, where_ref, near_ref, degree_ref, self_ref, base_ref, weight_ref, down_ref, own_ref,
    up_ref, *refs,
):
    done, (home_ref, away_ref) = refs[:-2], refs[-2:]
    for earlier in range(layer + 1):
        for core in range(2):
            if (earlier, core) == (layer, 1):
                continue
            ref = done[2 * earlier + core]

            @pl.when(at(where_ref, earlier, core))
            def _():
                home_ref[...] = ref[pl.ds(core * BLOCK, BLOCK), :]
                away_ref[...] = ref[pl.ds((1 - core) * BLOCK, BLOCK), :]

    @pl.when(at(where_ref, layer, 1))
    def _():
        rows = fresh_rows(down_ref, own_ref, up_ref)
        summed = dot(near_ref[...], rows) + base_ref[...]
        made = finish(summed, degree_ref, self_ref, weight_ref)
        home_ref[...] = made[BLOCK:]
        away_ref[...] = made[:BLOCK]


def leave_kernel(where_ref, home_ref, arrived_ref, result_ref, sems):
    for core in range(2):

        @pl.when(where_ref[1] == core)
        def _():
            copies = [
                pltpu.make_async_copy(
                    ref, result_ref.at[pl.ds(slab * BLOCK, BLOCK), :], sems.at[slab]
                )
                for slab, ref in ((core, home_ref), (1 - core, arrived_ref))
            ]
            for copy in copies:
                copy.start()
            for copy in copies:
                copy.wait()


def call(kernel, outs, *args, label, **extra):
    options = dict(compiler_params=params(), cost_estimate=COST, name=label)
    options.update(extra)
    specs = [SMEM if a.dtype == jnp.int32 and a.size < 128 else VMEM for a in args]
    options.setdefault("out_specs", [VMEM] * len(outs))
    return pl.pallas_call(kernel, out_shape=outs, in_specs=specs, **options)(*args)


def per_device(stacked, edges, picks, self_w, neigh_w):
    layers, domains = lax.axis_size("section"), lax.axis_size("dom")
    width = stacked.shape[2]
    mine = stacked[0]
    weight_self, weight_neigh = self_w[0], neigh_w[0]
    where = jnp.stack([lax.axis_index("section"), lax.axis_index("dom") % 2]).astype(jnp.int32)

    def bf16(rows, columns=width):
        return jax.ShapeDtypeStruct((rows, columns), jnp.bfloat16)

    def f32(rows, columns=width):
        return jax.ShapeDtypeStruct((rows, columns), jnp.float32)

    def route(value, jump, cores, sections, hop, label):
        pairs = [
            (s * domains + (d + jump(d)) % domains, (s + hop) * domains + d)
            for s in sections
            for d in range(domains)
            if d % 2 in cores
        ]
        with jax.named_scope(label):
            return lax.ppermute(value, ("section", "dom"), pairs)

    def steady(jump):
        return lambda d: jump

    def partner(d):
        return 1 if d % 2 == 0 else -1

    every = range(layers)
    both = (0, 1)
    up_mine = route(mine, steady(2), both, every, 0, "init_up")
    down_even = route(mine, steady(-1), (0,), every, 0, "init_down")
    other = route(mine, partner, both, every, 0, "init_other")
    (tiles,) = call(tiles_kernel, [bf16(ROWS, 8 * BLOCK)], picks, edges, label="tiles")
    tiles_other = route(tiles, partner, both, every, 0, "init_tiles")
    near, far, lend, degree = call(
        weave_kernel,
        [bf16(ROWS, SPAN)] * 3 + [f32(ROWS, 128)],
        where, tiles, tiles_other,
        label="weave",
    )
    (part,) = call(first_self_kernel, [f32(ROWS)], where, weight_self, mine, other, label="self0")
    up_other = route(up_mine, partner, both, every, 0, "init_up_other")
    down_odd = route(down_even, partner, (1,), [0], 0, "init_down_odd")
    made, tail = [], []
    for core in range(2):
        m, t = call(
            functools.partial(first_kernel, core),
            [bf16(ROWS), bf16(BLOCK)],
            where, near, far, degree, part, weight_neigh,
            down_odd if core else down_even, mine, other, up_mine, up_other,
            label="first",
        )
        made.append(m)
        tail.append(t)
    (base,) = call(
        history_kernel, [f32(ROWS)], where, far, down_even, mine, other, up_mine, up_other,
        label="history",
    )
    def send(rows, last_block, layer, core):
        cores, ends = (core,), [layer - 1]
        own = route(rows, steady(0), cores, ends, 1, f"own_l{layer}c{core}")
        up = route(rows, steady(2), cores, ends, 1, f"up_l{layer}c{core}")
        down = route(last_block, steady(-2), cores, ends, 1, f"down_l{layer}c{core}")
        return own, up, down

    done = list(made)
    tail[0], _ = lax.optimization_barrier((tail[0], down_odd))
    moving = [send(made[core], tail[core], 1, core) for core in range(2)]
    for layer in range(1, layers):
        (own, up, down), (own1, up1, down1) = moving
        with jax.named_scope(f"self_l{layer}c0"):
            (part,) = call(
                functools.partial(self_kernel, layer, 0), [f32(ROWS)], where, weight_self, own,
                label="self",
            )
        with jax.named_scope(f"slab0_l{layer}"):
            m0, t0, lent = call(
                functools.partial(slab0_kernel, layer),
                [bf16(ROWS), bf16(BLOCK), f32(ROWS)],
                where, near, lend, degree, part, base, weight_neigh, down, own, up,
                label="slab0",
            )
        done.append(m0)
        if layer < layers - 1:
            ahead = send(m0, t0, layer + 1, 0)
            lent, *ahead = lax.optimization_barrier((lent, *ahead))
        lent = route(lent, partner, (1,), [layer], 0, f"lent_l{layer}")
        with jax.named_scope(f"self_l{layer}c1"):
            (part,) = call(
                functools.partial(self_kernel, layer, 1), [f32(ROWS)], where, weight_self, own1,
                label="self",
            )
        inputs = (where, near, degree, part, lent, weight_neigh, down1, own1, up1)
        with jax.named_scope(f"slab1_l{layer}"):
            if layer < layers - 1:
                m1, t1 = call(
                    functools.partial(slab1_kernel, layer), [bf16(ROWS), bf16(BLOCK)], *inputs,
                    label="slab1",
                )
                done.append(m1)
                moving = [ahead, send(m1, t1, layer + 1, 1)]
            else:
                home, away = call(
                    functools.partial(last_kernel, layer), [bf16(BLOCK)] * 2, *inputs, *done,
                    label="last",
                )
    arrived = route(away, partner, both, every, 0, "last_swap")
    (result,) = call(
        leave_kernel,
        [bf16(ROWS)],
        where, home, arrived,
        label="leave",
        out_specs=[ANY],
        scratch_shapes=[pltpu.SemaphoreType.DMA((2,))],
    )
    return result[None]


def solution(mesh):
    in_specs = (
        P("section", "dom", None),
        P("dom", None),
        P("dom", None),
        P("section", None, None),
        P("section", None, None),
    )
    out_specs = P("section", "dom", None)
    return jax.shard_map(
        per_device, mesh=mesh, in_specs=in_specs, out_specs=out_specs, check_vma=False
    )
```

```python
import functools

import jax
import jax.numpy as jnp
from jax import lax
from jax.experimental import pallas as pl
from jax.experimental.pallas import tpu as pltpu
from jax.sharding import PartitionSpec as P

BLOCK = 64
ROWS = 2 * BLOCK
SPAN = 6 * BLOCK
VMEM = pl.BlockSpec(memory_space=pltpu.VMEM)
SMEM = pl.BlockSpec(memory_space=pltpu.SMEM)
COST = pl.CostEstimate(flops=1_000_000_000, bytes_accessed=0, transcendentals=0)


def params():
    return pltpu.CompilerParams(vmem_limit_bytes=32 * 1024 * 1024)


def at(where_ref, section, core):
    return (where_ref[0] == section) & (where_ref[1] == core)


def dot(a, b):
    return jnp.dot(a, b, preferred_element_type=jnp.float32)


def tiles_kernel(picks_ref, edges_ref, tiles_ref):
    for slab in range(2):
        rows = pl.ds(slab * BLOCK, BLOCK)
        e = edges_ref[rows, :].astype(jnp.float32)
        columns = [e[:, :BLOCK]]
        for wanted in range(2):
            for k in range(3):
                live = jnp.where(picks_ref[slab, k] == wanted, 1.0, 0.0)
                columns.append(e[:, (k + 1) * BLOCK : (k + 2) * BLOCK] * live)
        columns.append(jnp.zeros_like(columns[0]))
        tiles_ref[rows, :] = jnp.concatenate(columns, axis=1).astype(jnp.bfloat16)


def weave_kernel(where_ref, mine_ref, other_ref, near_ref, far_ref, lend_ref, degree_ref):
    for core in range(2):
        even_ref, odd_ref = (mine_ref, other_ref) if core == 0 else (other_ref, mine_ref)

        @pl.when(where_ref[1] == core)
        def _():
            def put(out_ref, to_slab, from_slab):
                for r, ref in enumerate((even_ref, odd_ref)):
                    t = ref[pl.ds(to_slab * BLOCK, BLOCK), :].astype(jnp.float32)
                    part = [t[:, i * BLOCK : (i + 1) * BLOCK] for i in range(7)]
                    none = jnp.zeros_like(part[0])
                    behind, ahead, ahead2 = part[1 + 3 * from_slab : 4 + 3 * from_slab]
                    own = part[0] if to_slab == from_slab else none
                    five = [behind, own, ahead, ahead2, none]
                    columns = five + [none] if r == 0 else [none] + five
                    out_ref[pl.ds(r * BLOCK, BLOCK), :] = jnp.concatenate(columns, axis=1).astype(
                        jnp.bfloat16
                    )

            put(near_ref, core, core)
            put(far_ref, core, 1 - core)
            put(lend_ref, 1, 0)
            for r, ref in enumerate((even_ref, odd_ref)):
                t = ref[pl.ds(core * BLOCK, BLOCK), :].astype(jnp.float32)
                degree = 1.0 + jnp.sum(t, axis=1, keepdims=True)
                degree_ref[pl.ds(r * BLOCK, BLOCK), :] = jnp.broadcast_to(degree, (BLOCK, 128))


def staged_rows(core, slab, refs):
    down, mine, other, up_mine, up_other = refs
    if core == 0:
        order = (down, mine, other, up_mine, up_other, down)
    else:
        order = (down, other, mine, up_other, up_mine, down)
    return jnp.concatenate([ref[pl.ds(slab * BLOCK, BLOCK), :] for ref in order], axis=0)


def finish(summed, degree_ref, self_ref, weight_ref):
    mean_rows = (summed / degree_ref[:, :1]).astype(jnp.bfloat16)
    hidden = self_ref[...] + dot(mean_rows, weight_ref[...])
    return jnp.maximum(hidden, 0.0).astype(jnp.bfloat16)


def first_self_kernel(where_ref, weight_ref, mine_ref, other_ref, out_ref):
    for core in range(2):
        even_ref, odd_ref = (mine_ref, other_ref) if core == 0 else (other_ref, mine_ref)

        @pl.when(at(where_ref, 0, core))
        def _():
            rows = pl.ds(core * BLOCK, BLOCK)
            own = jnp.concatenate([even_ref[rows, :], odd_ref[rows, :]], axis=0)
            out_ref[...] = dot(own, weight_ref[...])


def first_kernel(
    core, where_ref, near_ref, far_ref, degree_ref, self_ref, weight_ref, down_ref, mine_ref,
    other_ref, up_mine_ref, up_other_ref, made_ref, tail_ref,
):
    refs = (down_ref, mine_ref, other_ref, up_mine_ref, up_other_ref)

    @pl.when(at(where_ref, 0, core))
    def _():
        summed = dot(near_ref[...], staged_rows(core, core, refs))
        summed = summed + dot(far_ref[...], staged_rows(core, 1 - core, refs))
        made = finish(summed, degree_ref, self_ref, weight_ref)
        made_ref[...] = made
        tail_ref[...] = made[BLOCK:]


def history_kernel(
    where_ref, far_ref, down_ref, mine_ref, other_ref, up_mine_ref, up_other_ref, out_ref
):
    refs = (down_ref, mine_ref, other_ref, up_mine_ref, up_other_ref)

    @pl.when((where_ref[0] > 0) & (where_ref[1] == 0))
    def _():
        out_ref[...] = dot(far_ref[...], staged_rows(0, 1, refs))


def self_kernel(layer, core, where_ref, weight_ref, own_ref, out_ref):
    @pl.when(at(where_ref, layer, core))
    def _():
        out_ref[...] = dot(own_ref[...], weight_ref[...])


def fresh_rows(down_ref, own_ref, up_ref):
    return jnp.concatenate([down_ref[...], own_ref[...], up_ref[...], down_ref[...]], axis=0)


def slab0_kernel(
    layer, where_ref, near_ref, lend_ref, degree_ref, self_ref, base_ref, weight_ref, down_ref,
    own_ref, up_ref, made_ref, tail_ref, lent_ref,
):
    @pl.when(at(where_ref, layer, 0))
    def _():
        rows = fresh_rows(down_ref, own_ref, up_ref)
        summed = dot(near_ref[...], rows) + base_ref[...]
        made = finish(summed, degree_ref, self_ref, weight_ref)
        made_ref[...] = made
        tail_ref[...] = made[BLOCK:]
        lent_ref[...] = dot(lend_ref[...], rows)


def slab1_kernel(
    layer, where_ref, near_ref, degree_ref, self_ref, base_ref, weight_ref, down_ref, own_ref,
    up_ref, made_ref, tail_ref,
):
    @pl.when(at(where_ref, layer, 1))
    def _():
        rows = fresh_rows(down_ref, own_ref, up_ref)
        summed = dot(near_ref[...], rows) + base_ref[...]
        made = finish(summed, degree_ref, self_ref, weight_ref)
        made_ref[...] = made
        tail_ref[...] = made[BLOCK:]


def last_kernel(
    layer, where_ref, near_ref, degree_ref, self_ref, base_ref, weight_ref, down_ref, own_ref,
    up_ref, *refs,
):
    done, (home_ref, away_ref) = refs[:-2], refs[-2:]
    for earlier in range(layer + 1):
        for core in range(2):
            if (earlier, core) == (layer, 1):
                continue
            ref = done[2 * earlier + core]

            @pl.when(at(where_ref, earlier, core))
            def _():
                home_ref[...] = ref[pl.ds(core * BLOCK, BLOCK), :]
                away_ref[...] = ref[pl.ds((1 - core) * BLOCK, BLOCK), :]

    @pl.when(at(where_ref, layer, 1))
    def _():
        rows = fresh_rows(down_ref, own_ref, up_ref)
        summed = dot(near_ref[...], rows) + base_ref[...]
        made = finish(summed, degree_ref, self_ref, weight_ref)
        home_ref[...] = made[BLOCK:]
        away_ref[...] = made[:BLOCK]


def call(kernel, outs, *args, label, **extra):
    options = dict(compiler_params=params(), cost_estimate=COST, name=label)
    options.update(extra)
    specs = [SMEM if a.dtype == jnp.int32 and a.size < 128 else VMEM for a in args]
    options.setdefault("out_specs", [VMEM] * len(outs))
    return pl.pallas_call(kernel, out_shape=outs, in_specs=specs, **options)(*args)


def per_device(stacked, edges, picks, self_w, neigh_w):
    layers, domains = lax.axis_size("section"), lax.axis_size("dom")
    width = stacked.shape[2]
    mine = stacked[0]
    weight_self, weight_neigh = self_w[0], neigh_w[0]
    where = jnp.stack([lax.axis_index("section"), lax.axis_index("dom") % 2]).astype(jnp.int32)

    def bf16(rows, columns=width):
        return jax.ShapeDtypeStruct((rows, columns), jnp.bfloat16)

    def f32(rows, columns=width):
        return jax.ShapeDtypeStruct((rows, columns), jnp.float32)

    def route(value, jump, cores, sections, hop, label):
        pairs = [
            (s * domains + (d + jump(d)) % domains, (s + hop) * domains + d)
            for s in sections
            for d in range(domains)
            if d % 2 in cores
        ]
        with jax.named_scope(label):
            return lax.ppermute(value, ("section", "dom"), pairs)

    def steady(jump):
        return lambda d: jump

    def partner(d):
        return 1 if d % 2 == 0 else -1

    every = range(layers)
    both = (0, 1)
    up_mine = route(mine, steady(2), both, every, 0, "init_up")
    down_even = route(mine, steady(-1), (0,), every, 0, "init_down")
    (tiles,) = call(tiles_kernel, [bf16(ROWS, 8 * BLOCK)], picks, edges, label="tiles")
    held, tiles = lax.optimization_barrier((mine, tiles))
    other = route(held, partner, both, every, 0, "init_other")
    tiles_other = route(tiles, partner, both, every, 0, "init_tiles")
    near, far, lend, degree = call(
        weave_kernel,
        [bf16(ROWS, SPAN)] * 3 + [f32(ROWS, 128)],
        where, tiles, tiles_other,
        label="weave",
    )
    (part,) = call(first_self_kernel, [f32(ROWS)], where, weight_self, mine, other, label="self0")
    up_other = route(up_mine, partner, both, every, 0, "init_up_other")
    down_odd = route(down_even, partner, (1,), [0], 0, "init_down_odd")
    made, tail = [], []
    for core in range(2):
        m, t = call(
            functools.partial(first_kernel, core),
            [bf16(ROWS), bf16(BLOCK)],
            where, near, far, degree, part, weight_neigh,
            down_odd if core else down_even, mine, other, up_mine, up_other,
            label="first",
        )
        made.append(m)
        tail.append(t)
    (base,) = call(
        history_kernel, [f32(ROWS)], where, far, down_even, mine, other, up_mine, up_other,
        label="history",
    )
    def send(rows, last_block, layer, core):
        cores, ends = (core,), [layer - 1]
        own = route(rows, steady(0), cores, ends, 1, f"own_l{layer}c{core}")
        up = route(rows, steady(2), cores, ends, 1, f"up_l{layer}c{core}")
        down = route(last_block, steady(-2), cores, ends, 1, f"down_l{layer}c{core}")
        return own, up, down

    done = list(made)
    tail[0], _ = lax.optimization_barrier((tail[0], down_odd))
    moving = [send(made[core], tail[core], 1, core) for core in range(2)]
    for layer in range(1, layers):
        (own, up, down), (own1, up1, down1) = moving
        with jax.named_scope(f"self_l{layer}c0"):
            (part,) = call(
                functools.partial(self_kernel, layer, 0), [f32(ROWS)], where, weight_self, own,
                label="self",
            )
        with jax.named_scope(f"slab0_l{layer}"):
            m0, t0, lent = call(
                functools.partial(slab0_kernel, layer),
                [bf16(ROWS), bf16(BLOCK), f32(ROWS)],
                where, near, lend, degree, part, base, weight_neigh, down, own, up,
                label="slab0",
            )
        done.append(m0)
        if layer < layers - 1:
            ahead = send(m0, t0, layer + 1, 0)
            if layer > 1:
                lent, *ahead = lax.optimization_barrier((lent, *ahead))
        lent = route(lent, partner, (1,), [layer], 0, f"lent_l{layer}")
        with jax.named_scope(f"self_l{layer}c1"):
            (part,) = call(
                functools.partial(self_kernel, layer, 1), [f32(ROWS)], where, weight_self, own1,
                label="self",
            )
        inputs = (where, near, degree, part, lent, weight_neigh, down1, own1, up1)
        with jax.named_scope(f"slab1_l{layer}"):
            if layer < layers - 1:
                m1, t1 = call(
                    functools.partial(slab1_kernel, layer), [bf16(ROWS), bf16(BLOCK)], *inputs,
                    label="slab1",
                )
                done.append(m1)
                moving = [ahead, send(m1, t1, layer + 1, 1)]
            else:
                home, away = call(
                    functools.partial(last_kernel, layer), [bf16(BLOCK)] * 2, *inputs, *done,
                    label="last",
                )
    arrived = route(away, partner, both, every, 0, "last_swap")
    even = where[1] == 0
    rows = [jnp.where(even, home, arrived), jnp.where(even, arrived, home)]
    result = jnp.concatenate(rows, axis=0)
    return result[None]


def solution(mesh):
    in_specs = (
        P("section", "dom", None),
        P("dom", None),
        P("dom", None),
        P("section", None, None),
        P("section", None, None),
    )
    out_specs = P("section", "dom", None)
    return jax.shard_map(
        per_device, mesh=mesh, in_specs=in_specs, out_specs=out_specs, check_vma=False
    )
```

```python
import functools

import jax
import jax.numpy as jnp
from jax import lax
from jax.experimental import pallas as pl
from jax.experimental.pallas import tpu as pltpu
from jax.sharding import PartitionSpec as P

BLOCK = 64
ROWS = 2 * BLOCK
SPAN = 6 * BLOCK
VMEM = pl.BlockSpec(memory_space=pltpu.VMEM)
SMEM = pl.BlockSpec(memory_space=pltpu.SMEM)
COST = pl.CostEstimate(flops=1_000_000_000, bytes_accessed=0, transcendentals=0)


def params():
    return pltpu.CompilerParams(vmem_limit_bytes=32 * 1024 * 1024)


def at(where_ref, section, core):
    return (where_ref[0] == section) & (where_ref[1] == core)


def dot(a, b):
    return jnp.dot(a, b, preferred_element_type=jnp.float32)


def tiles_kernel(picks_ref, edges_ref, tiles_ref):
    for slab in range(2):
        rows = pl.ds(slab * BLOCK, BLOCK)
        e = edges_ref[rows, :].astype(jnp.float32)
        columns = [e[:, :BLOCK]]
        for wanted in range(2):
            for k in range(3):
                live = jnp.where(picks_ref[slab, k] == wanted, 1.0, 0.0)
                columns.append(e[:, (k + 1) * BLOCK : (k + 2) * BLOCK] * live)
        columns.append(jnp.zeros_like(columns[0]))
        tiles_ref[rows, :] = jnp.concatenate(columns, axis=1).astype(jnp.bfloat16)


def weave_kernel(where_ref, mine_ref, other_ref, near_ref, far_ref, lend_ref, degree_ref):
    for core in range(2):
        even_ref, odd_ref = (mine_ref, other_ref) if core == 0 else (other_ref, mine_ref)

        @pl.when(where_ref[1] == core)
        def _():
            def put(out_ref, to_slab, from_slab):
                for r, ref in enumerate((even_ref, odd_ref)):
                    t = ref[pl.ds(to_slab * BLOCK, BLOCK), :].astype(jnp.float32)
                    part = [t[:, i * BLOCK : (i + 1) * BLOCK] for i in range(7)]
                    none = jnp.zeros_like(part[0])
                    behind, ahead, ahead2 = part[1 + 3 * from_slab : 4 + 3 * from_slab]
                    own = part[0] if to_slab == from_slab else none
                    five = [behind, own, ahead, ahead2, none]
                    columns = five + [none] if r == 0 else [none] + five
                    out_ref[pl.ds(r * BLOCK, BLOCK), :] = jnp.concatenate(columns, axis=1).astype(
                        jnp.bfloat16
                    )

            put(near_ref, core, core)
            put(far_ref, core, 1 - core)
            put(lend_ref, 1, 0)
            for r, ref in enumerate((even_ref, odd_ref)):
                t = ref[pl.ds(core * BLOCK, BLOCK), :].astype(jnp.float32)
                degree = 1.0 + jnp.sum(t, axis=1, keepdims=True)
                degree_ref[pl.ds(r * BLOCK, BLOCK), :] = jnp.broadcast_to(degree, (BLOCK, 128))


def staged_rows(core, slab, refs):
    down, mine, other, up_mine, up_other = refs
    if core == 0:
        order = (down, mine, other, up_mine, up_other, down)
    else:
        order = (down, other, mine, up_other, up_mine, down)
    return jnp.concatenate([ref[pl.ds(slab * BLOCK, BLOCK), :] for ref in order], axis=0)


def finish(summed, degree_ref, self_part, weight_ref):
    mean_rows = (summed / degree_ref[:, :1]).astype(jnp.bfloat16)
    hidden = self_part + dot(mean_rows, weight_ref[...])
    return jnp.maximum(hidden, 0.0).astype(jnp.bfloat16)


def first_self_kernel(where_ref, weight_ref, mine_ref, other_ref, out_ref):
    for core in range(2):
        even_ref, odd_ref = (mine_ref, other_ref) if core == 0 else (other_ref, mine_ref)

        @pl.when(at(where_ref, 0, core))
        def _():
            rows = pl.ds(core * BLOCK, BLOCK)
            own = jnp.concatenate([even_ref[rows, :], odd_ref[rows, :]], axis=0)
            out_ref[...] = dot(own, weight_ref[...])


def first_kernel(
    core, where_ref, near_ref, far_ref, degree_ref, self_ref, weight_ref, down_ref, mine_ref,
    other_ref, up_mine_ref, up_other_ref, made_ref, tail_ref,
):
    refs = (down_ref, mine_ref, other_ref, up_mine_ref, up_other_ref)

    @pl.when(at(where_ref, 0, core))
    def _():
        summed = dot(near_ref[...], staged_rows(core, core, refs))
        summed = summed + dot(far_ref[...], staged_rows(core, 1 - core, refs))
        made = finish(summed, degree_ref, self_ref[...], weight_ref)
        made_ref[...] = made
        tail_ref[...] = made[BLOCK:]


def history_kernel(
    where_ref, far_ref, down_ref, mine_ref, other_ref, up_mine_ref, up_other_ref, out_ref
):
    refs = (down_ref, mine_ref, other_ref, up_mine_ref, up_other_ref)

    @pl.when((where_ref[0] > 0) & (where_ref[1] == 0))
    def _():
        out_ref[...] = dot(far_ref[...], staged_rows(0, 1, refs))


def fresh_rows(down_ref, own_ref, up_ref):
    return jnp.concatenate([down_ref[...], own_ref[...], up_ref[...], down_ref[...]], axis=0)


def slab0_kernel(
    layer, where_ref, near_ref, lend_ref, degree_ref, self_ref, base_ref, weight_ref, up_ref,
    down_ref, own_ref, made_ref, tail_ref, lent_ref,
):
    @pl.when(at(where_ref, layer, 0))
    def _():
        rows = fresh_rows(down_ref, own_ref, up_ref)
        summed = dot(near_ref[...], rows) + base_ref[...]
        made = finish(summed, degree_ref, dot(own_ref[...], self_ref[...]), weight_ref)
        made_ref[...] = made
        tail_ref[...] = made[BLOCK:]
        lent_ref[...] = dot(lend_ref[...], rows)


def slab1_kernel(
    layer, where_ref, near_ref, degree_ref, self_ref, base_ref, weight_ref, up_ref, down_ref,
    own_ref, made_ref, tail_ref,
):
    @pl.when(at(where_ref, layer, 1))
    def _():
        rows = fresh_rows(down_ref, own_ref, up_ref)
        summed = dot(near_ref[...], rows) + base_ref[...]
        made = finish(summed, degree_ref, dot(own_ref[...], self_ref[...]), weight_ref)
        made_ref[...] = made
        tail_ref[...] = made[BLOCK:]


def last_kernel(
    layer, where_ref, near_ref, degree_ref, self_ref, base_ref, weight_ref, up_ref, down_ref,
    own_ref, *refs,
):
    done, (home_ref, away_ref) = refs[:-2], refs[-2:]
    for earlier in range(layer + 1):
        for core in range(2):
            if (earlier, core) == (layer, 1):
                continue
            ref = done[2 * earlier + core]

            @pl.when(at(where_ref, earlier, core))
            def _():
                home_ref[...] = ref[pl.ds(core * BLOCK, BLOCK), :]
                away_ref[...] = ref[pl.ds((1 - core) * BLOCK, BLOCK), :]

    @pl.when(at(where_ref, layer, 1))
    def _():
        rows = fresh_rows(down_ref, own_ref, up_ref)
        summed = dot(near_ref[...], rows) + base_ref[...]
        made = finish(summed, degree_ref, dot(own_ref[...], self_ref[...]), weight_ref)
        home_ref[...] = made[BLOCK:]
        away_ref[...] = made[:BLOCK]


def call(kernel, outs, *args, label, **extra):
    options = dict(compiler_params=params(), cost_estimate=COST, name=label)
    options.update(extra)
    specs = [SMEM if a.dtype == jnp.int32 and a.size < 128 else VMEM for a in args]
    options.setdefault("out_specs", [VMEM] * len(outs))
    return pl.pallas_call(kernel, out_shape=outs, in_specs=specs, **options)(*args)


def per_device(stacked, edges, picks, self_w, neigh_w):
    layers, domains = lax.axis_size("section"), lax.axis_size("dom")
    width = stacked.shape[2]
    mine = stacked[0]
    weight_self, weight_neigh = self_w[0], neigh_w[0]
    where = jnp.stack([lax.axis_index("section"), lax.axis_index("dom") % 2]).astype(jnp.int32)

    def bf16(rows, columns=width):
        return jax.ShapeDtypeStruct((rows, columns), jnp.bfloat16)

    def f32(rows, columns=width):
        return jax.ShapeDtypeStruct((rows, columns), jnp.float32)

    def route(value, jump, cores, sections, hop, label):
        pairs = [
            (s * domains + (d + jump(d)) % domains, (s + hop) * domains + d)
            for s in sections
            for d in range(domains)
            if d % 2 in cores
        ]
        with jax.named_scope(label):
            return lax.ppermute(value, ("section", "dom"), pairs)

    def steady(jump):
        return lambda d: jump

    def partner(d):
        return 1 if d % 2 == 0 else -1

    every = range(layers)
    both = (0, 1)
    up_mine = route(mine, steady(2), both, every, 0, "init_up")
    down_even = route(mine, steady(-1), (0,), every, 0, "init_down")
    (tiles,) = call(tiles_kernel, [bf16(ROWS, 8 * BLOCK)], picks, edges, label="tiles")
    held, tiles = lax.optimization_barrier((mine, tiles))
    other = route(held, partner, both, every, 0, "init_other")
    tiles_other = route(tiles, partner, both, every, 0, "init_tiles")
    near, far, lend, degree = call(
        weave_kernel,
        [bf16(ROWS, SPAN)] * 3 + [f32(ROWS, 128)],
        where, tiles, tiles_other,
        label="weave",
    )
    (part,) = call(first_self_kernel, [f32(ROWS)], where, weight_self, mine, other, label="self0")
    up_other = route(up_mine, partner, both, every, 0, "init_up_other")
    down_odd = route(down_even, partner, (1,), [0], 0, "init_down_odd")
    made, tail = [], []
    for core in range(2):
        m, t = call(
            functools.partial(first_kernel, core),
            [bf16(ROWS), bf16(BLOCK)],
            where, near, far, degree, part, weight_neigh,
            down_odd if core else down_even, mine, other, up_mine, up_other,
            label="first",
        )
        made.append(m)
        tail.append(t)
    (base,) = call(
        history_kernel, [f32(ROWS)], where, far, down_even, mine, other, up_mine, up_other,
        label="history",
    )
    def send(rows, last_block, layer, core):
        cores, ends = (core,), [layer - 1]
        own = route(rows, steady(0), cores, ends, 1, f"own_l{layer}c{core}")
        up = route(rows, steady(2), cores, ends, 1, f"up_l{layer}c{core}")
        down = route(last_block, steady(-2), cores, ends, 1, f"down_l{layer}c{core}")
        return own, up, down

    done = list(made)
    tail[0], _ = lax.optimization_barrier((tail[0], down_odd))
    moving = [send(made[core], tail[core], 1, core) for core in range(2)]
    for layer in range(1, layers):
        (own, up, down), (own1, up1, down1) = moving
        with jax.named_scope(f"slab0_l{layer}"):
            m0, t0, lent = call(
                functools.partial(slab0_kernel, layer),
                [bf16(ROWS), bf16(BLOCK), f32(ROWS)],
                where, near, lend, degree, weight_self, base, weight_neigh, up, down, own,
                label="slab0",
            )
        done.append(m0)
        if layer < layers - 1:
            ahead = send(m0, t0, layer + 1, 0)
            if layer > 1:
                lent, *ahead = lax.optimization_barrier((lent, *ahead))
        lent = route(lent, partner, (1,), [layer], 0, f"lent_l{layer}")
        inputs = (where, near, degree, weight_self, lent, weight_neigh, up1, down1, own1)
        with jax.named_scope(f"slab1_l{layer}"):
            if layer < layers - 1:
                m1, t1 = call(
                    functools.partial(slab1_kernel, layer), [bf16(ROWS), bf16(BLOCK)], *inputs,
                    label="slab1",
                )
                done.append(m1)
                moving = [ahead, send(m1, t1, layer + 1, 1)]
            else:
                home, away = call(
                    functools.partial(last_kernel, layer), [bf16(BLOCK)] * 2, *inputs, *done,
                    label="last",
                )
    arrived = route(away, partner, both, every, 0, "last_swap")
    even = where[1] == 0
    rows = [jnp.where(even, home, arrived), jnp.where(even, arrived, home)]
    result = jnp.concatenate(rows, axis=0)
    return result[None]


def solution(mesh):
    in_specs = (
        P("section", "dom", None),
        P("dom", None),
        P("dom", None),
        P("section", None, None),
        P("section", None, None),
    )
    out_specs = P("section", "dom", None)
    return jax.shard_map(
        per_device, mesh=mesh, in_specs=in_specs, out_specs=out_specs, check_vma=False
    )
```

```python
import functools

import jax
import jax.numpy as jnp
from jax import lax
from jax.experimental import pallas as pl
from jax.experimental.pallas import tpu as pltpu
from jax.sharding import PartitionSpec as P

BLOCK = 64
ROWS = 2 * BLOCK
SPAN = 6 * BLOCK
VMEM = pl.BlockSpec(memory_space=pltpu.VMEM)
SMEM = pl.BlockSpec(memory_space=pltpu.SMEM)
COST = pl.CostEstimate(flops=1_000_000_000, bytes_accessed=0, transcendentals=0)


def params():
    return pltpu.CompilerParams(vmem_limit_bytes=32 * 1024 * 1024)


def at(where_ref, section, core):
    return (where_ref[0] == section) & (where_ref[1] == core)


def dot(a, b):
    return jnp.dot(a, b, preferred_element_type=jnp.float32)


def tiles_kernel(picks_ref, edges_ref, tiles_ref):
    for slab in range(2):
        rows = pl.ds(slab * BLOCK, BLOCK)
        e = edges_ref[rows, :].astype(jnp.float32)
        columns = [e[:, :BLOCK]]
        for wanted in range(2):
            for k in range(3):
                live = jnp.where(picks_ref[slab, k] == wanted, 1.0, 0.0)
                columns.append(e[:, (k + 1) * BLOCK : (k + 2) * BLOCK] * live)
        columns.append(jnp.zeros_like(columns[0]))
        tiles_ref[rows, :] = jnp.concatenate(columns, axis=1).astype(jnp.bfloat16)


def weave_kernel(where_ref, mine_ref, other_ref, near_ref, far_ref, lend_ref, degree_ref):
    for core in range(2):
        even_ref, odd_ref = (mine_ref, other_ref) if core == 0 else (other_ref, mine_ref)

        @pl.when(where_ref[1] == core)
        def _():
            def put(out_ref, to_slab, from_slab):
                for r, ref in enumerate((even_ref, odd_ref)):
                    t = ref[pl.ds(to_slab * BLOCK, BLOCK), :].astype(jnp.float32)
                    part = [t[:, i * BLOCK : (i + 1) * BLOCK] for i in range(7)]
                    none = jnp.zeros_like(part[0])
                    behind, ahead, ahead2 = part[1 + 3 * from_slab : 4 + 3 * from_slab]
                    own = part[0] if to_slab == from_slab else none
                    five = [behind, own, ahead, ahead2, none]
                    columns = five + [none] if r == 0 else [none] + five
                    out_ref[pl.ds(r * BLOCK, BLOCK), :] = jnp.concatenate(columns, axis=1).astype(
                        jnp.bfloat16
                    )

            put(near_ref, core, core)
            put(far_ref, core, 1 - core)
            put(lend_ref, 1, 0)
            for r, ref in enumerate((even_ref, odd_ref)):
                t = ref[pl.ds(core * BLOCK, BLOCK), :].astype(jnp.float32)
                degree = 1.0 + jnp.sum(t, axis=1, keepdims=True)
                degree_ref[pl.ds(r * BLOCK, BLOCK), :] = jnp.broadcast_to(degree, (BLOCK, 128))


def staged_rows(core, slab, refs):
    down, mine, other, up_mine, up_other = refs
    if core == 0:
        order = (down, mine, other, up_mine, up_other, down)
    else:
        order = (down, other, mine, up_other, up_mine, down)
    return jnp.concatenate([ref[pl.ds(slab * BLOCK, BLOCK), :] for ref in order], axis=0)


def finish(summed, degree_ref, self_part, weight_ref):
    mean_rows = (summed / degree_ref[:, :1]).astype(jnp.bfloat16)
    hidden = self_part + dot(mean_rows, weight_ref[...])
    return jnp.maximum(hidden, 0.0).astype(jnp.bfloat16)


def first_self_kernel(where_ref, weight_ref, mine_ref, other_ref, out_ref):
    for core in range(2):
        even_ref, odd_ref = (mine_ref, other_ref) if core == 0 else (other_ref, mine_ref)

        @pl.when(at(where_ref, 0, core))
        def _():
            rows = pl.ds(core * BLOCK, BLOCK)
            own = jnp.concatenate([even_ref[rows, :], odd_ref[rows, :]], axis=0)
            out_ref[...] = dot(own, weight_ref[...])


def first_kernel(
    core, where_ref, near_ref, far_ref, degree_ref, self_ref, weight_ref, down_ref, mine_ref,
    other_ref, up_mine_ref, up_other_ref, made_ref, tail_ref,
):
    refs = (down_ref, mine_ref, other_ref, up_mine_ref, up_other_ref)

    @pl.when(at(where_ref, 0, core))
    def _():
        summed = dot(near_ref[...], staged_rows(core, core, refs))
        summed = summed + dot(far_ref[...], staged_rows(core, 1 - core, refs))
        made = finish(summed, degree_ref, self_ref[...], weight_ref)
        made_ref[...] = made
        tail_ref[...] = made[BLOCK:]


def history_kernel(
    where_ref, far_ref, down_ref, mine_ref, other_ref, up_mine_ref, up_other_ref, out_ref
):
    refs = (down_ref, mine_ref, other_ref, up_mine_ref, up_other_ref)

    @pl.when((where_ref[0] > 0) & (where_ref[1] == 0))
    def _():
        out_ref[...] = dot(far_ref[...], staged_rows(0, 1, refs))


def fresh_rows(down_ref, own_ref, up_ref):
    return jnp.concatenate([down_ref[...], own_ref[...], up_ref[...], down_ref[...]], axis=0)


def slab0_kernel(
    layer, where_ref, near_ref, lend_ref, degree_ref, self_ref, base_ref, weight_ref, up_ref,
    down_ref, own_ref, made_ref, tail_ref, lent_ref,
):
    @pl.when(at(where_ref, layer, 0))
    def _():
        rows = fresh_rows(down_ref, own_ref, up_ref)
        summed = dot(near_ref[...], rows) + base_ref[...]
        made = finish(summed, degree_ref, dot(own_ref[...], self_ref[...]), weight_ref)
        made_ref[...] = made
        tail_ref[...] = made[BLOCK:]
        lent_ref[...] = dot(lend_ref[...], rows)


def slab1_kernel(
    layer, where_ref, near_ref, degree_ref, self_ref, base_ref, weight_ref, up_ref, down_ref,
    own_ref, made_ref, tail_ref,
):
    @pl.when(at(where_ref, layer, 1))
    def _():
        rows = fresh_rows(down_ref, own_ref, up_ref)
        summed = dot(near_ref[...], rows) + base_ref[...]
        made = finish(summed, degree_ref, dot(own_ref[...], self_ref[...]), weight_ref)
        made_ref[...] = made
        tail_ref[...] = made[BLOCK:]


def last_kernel(
    layer, where_ref, near_ref, degree_ref, self_ref, base_ref, weight_ref, up_ref, down_ref,
    own_ref, *refs,
):
    done, (home_ref, away_ref) = refs[:-2], refs[-2:]
    for earlier in range(layer + 1):
        for core in range(2):
            if (earlier, core) == (layer, 1):
                continue
            ref = done[2 * earlier + core]

            @pl.when(at(where_ref, earlier, core))
            def _():
                home_ref[...] = ref[pl.ds(core * BLOCK, BLOCK), :]
                away_ref[...] = ref[pl.ds((1 - core) * BLOCK, BLOCK), :]

    @pl.when(at(where_ref, layer, 1))
    def _():
        rows = fresh_rows(down_ref, own_ref, up_ref)
        summed = dot(near_ref[...], rows) + base_ref[...]
        made = finish(summed, degree_ref, dot(own_ref[...], self_ref[...]), weight_ref)
        home_ref[...] = made[BLOCK:]
        away_ref[...] = made[:BLOCK]


def call(kernel, outs, *args, label, **extra):
    options = dict(compiler_params=params(), cost_estimate=COST, name=label)
    options.update(extra)
    specs = [SMEM if a.dtype == jnp.int32 and a.size < 128 else VMEM for a in args]
    options.setdefault("out_specs", [VMEM] * len(outs))
    return pl.pallas_call(kernel, out_shape=outs, in_specs=specs, **options)(*args)


def per_device(stacked, edges, picks, self_w, neigh_w):
    layers, domains = lax.axis_size("section"), lax.axis_size("dom")
    width = stacked.shape[2]
    mine = stacked[0]
    weight_self, weight_neigh = self_w[0], neigh_w[0]
    where = jnp.stack([lax.axis_index("section"), lax.axis_index("dom") % 2]).astype(jnp.int32)

    def bf16(rows, columns=width):
        return jax.ShapeDtypeStruct((rows, columns), jnp.bfloat16)

    def f32(rows, columns=width):
        return jax.ShapeDtypeStruct((rows, columns), jnp.float32)

    def route(value, jump, cores, sections, hop, label):
        pairs = [
            (s * domains + (d + jump(d)) % domains, (s + hop) * domains + d)
            for s in sections
            for d in range(domains)
            if d % 2 in cores
        ]
        with jax.named_scope(label):
            return lax.ppermute(value, ("section", "dom"), pairs)

    def steady(jump):
        return lambda d: jump

    def partner(d):
        return 1 if d % 2 == 0 else -1

    every = range(layers)
    both = (0, 1)
    up_mine = route(mine, steady(2), both, every, 0, "init_up")
    down_even = route(mine, steady(-1), (0,), every, 0, "init_down")
    (tiles,) = call(tiles_kernel, [bf16(ROWS, 8 * BLOCK)], picks, edges, label="tiles")
    held, tiles = lax.optimization_barrier((mine, tiles))
    other = route(held, partner, both, every, 0, "init_other")
    tiles_other = route(tiles, partner, both, every, 0, "init_tiles")
    near, far, lend, degree = call(
        weave_kernel,
        [bf16(ROWS, SPAN)] * 3 + [f32(ROWS, 128)],
        where, tiles, tiles_other,
        label="weave",
    )
    (part,) = call(first_self_kernel, [f32(ROWS)], where, weight_self, mine, other, label="self0")
    up_other = route(up_mine, partner, both, every, 0, "init_up_other")
    down_odd = route(down_even, partner, (1,), [0], 0, "init_down_odd")
    made, tail = [], []
    for core in range(2):
        m, t = call(
            functools.partial(first_kernel, core),
            [bf16(ROWS), bf16(BLOCK)],
            where, near, far, degree, part, weight_neigh,
            down_odd if core else down_even, mine, other, up_mine, up_other,
            label="first",
        )
        made.append(m)
        tail.append(t)
    (base,) = call(
        history_kernel, [f32(ROWS)], where, far, down_even, mine, other, up_mine, up_other,
        label="history",
    )
    def send(rows, last_block, layer, core):
        cores, ends = (core,), [layer - 1]
        own = route(rows, steady(0), cores, ends, 1, f"own_l{layer}c{core}")
        up = route(rows, steady(2), cores, ends, 1, f"up_l{layer}c{core}")
        down = route(last_block, steady(-2), cores, ends, 1, f"down_l{layer}c{core}")
        return own, up, down

    done = list(made)
    tail[0], _ = lax.optimization_barrier((tail[0], down_odd))
    moving = [send(made[core], tail[core], 1, core) for core in range(2)]
    for layer in range(1, layers):
        (own, up, down), (own1, up1, down1) = moving
        with jax.named_scope(f"slab0_l{layer}"):
            m0, t0, lent = call(
                functools.partial(slab0_kernel, layer),
                [bf16(ROWS), bf16(BLOCK), f32(ROWS)],
                where, near, lend, degree, weight_self, base, weight_neigh, up, down, own,
                label="slab0",
            )
        done.append(m0)
        if layer < layers - 1:
            ahead = send(m0, t0, layer + 1, 0)
        lent = route(lent, partner, (1,), [layer], 0, f"lent_l{layer}")
        inputs = (where, near, degree, weight_self, lent, weight_neigh, up1, down1, own1)
        with jax.named_scope(f"slab1_l{layer}"):
            if layer < layers - 1:
                m1, t1 = call(
                    functools.partial(slab1_kernel, layer), [bf16(ROWS), bf16(BLOCK)], *inputs,
                    label="slab1",
                )
                done.append(m1)
                moving = [ahead, send(m1, t1, layer + 1, 1)]
            else:
                home, away = call(
                    functools.partial(last_kernel, layer), [bf16(BLOCK)] * 2, *inputs, *done,
                    label="last",
                )
    arrived = route(away, partner, both, every, 0, "last_swap")
    even = where[1] == 0
    rows = [jnp.where(even, home, arrived), jnp.where(even, arrived, home)]
    result = jnp.concatenate(rows, axis=0)
    return result[None]


def solution(mesh):
    in_specs = (
        P("section", "dom", None),
        P("dom", None),
        P("dom", None),
        P("section", None, None),
        P("section", None, None),
    )
    out_specs = P("section", "dom", None)
    return jax.shard_map(
        per_device, mesh=mesh, in_specs=in_specs, out_specs=out_specs, check_vma=False
    )
```
